32 devices in a mesh: leaf: 8 (over y, x, core), sub: 4 (over z).
Axes of the slice: x: 2, y: 2, z: 4, core: 2. Of those that a mesh axis runs over, the one named last changes fastest.
Arguments:
- densities: bfloat16 [16, 131072], P(None, ('leaf', 'sub')), may hold values from -6 to 6
- basis: bfloat16 [512, 64, 256], P(('leaf', 'sub')), may hold values from -0.375 to 0.375
- near_blocks: bfloat16 [512, 2048, 256], P(('leaf', 'sub')), may hold values from -0.125 to 0.125
- near_source: int32 [512, 8], P(('leaf', 'sub')), may hold values from 0 to 511, as said below
- near_valid: int32 [512, 8], P(('leaf', 'sub')), may hold values from 0 to 1
- leaf_coupling: bfloat16 [512, 64, 2048], P(('leaf', 'sub')), may hold values from -0.125 to 0.125
- leaf_source: int32 [512, 32], P(('leaf', 'sub')), may hold values from 0 to 511, as said below
- leaf_valid: int32 [512, 32], P(('leaf', 'sub')), may hold values from 0 to 1
- parent_transfer: bfloat16 [64, 64, 512], P(('leaf', 'sub')), may hold values from -0.4375 to 0.4375
- parent_coupling: bfloat16 [64, 64, 2048], P(('leaf', 'sub')), may hold values from -0.125 to 0.125
- parent_source: int32 [64, 32], P(('leaf', 'sub')), may hold values from 0 to 63
- parent_valid: int32 [64, 32], P(('leaf', 'sub')), may hold values 0 or 1
- grand_transfer: bfloat16 [8, 64, 512], replicated, may hold values from -0.4375 to 0.4375
- grand_coupling: bfloat16 [8, 64, 1024], P('leaf'), may hold values from -0.1875 to 0.1875
- grand_source: int32 [8, 16], P('leaf'), may hold values from 0 to 7
- grand_valid: int32 [8, 16], P('leaf'), may hold values 0 or 1
Outputs:
- potential: bfloat16 [16, 131072], P(None, ('leaf', 'sub'))
The draws below stay inside these ranges and needn't reach their ends.
Inputs may be any that keep to these rules, and one draw needn't show every extreme that they name: `leaf_source`: for the 16 leaves of one device (aligned blocks of rows), the slots with leaf_valid = 1 name leaves of any one aligned block of 16 leaves at most 32 times; this bound is reached in every draw. `near_source`: every near source leaf lies within 8 leaves of its target leaf in the curve order; both ends of the reach occur.
All inputs are finite; a program needn't handle non-finite values. No bound on the sum of `parent_valid` or of `grand_valid` on one device may be relied on, other than what follows from the above.
Results may differ from the reference program's by a relative error of at most 0.009.
Values may be sent and summed in bfloat16 or wider, within the bound.
A program may use at most 128 MiB of HBM per device.

```python
import math
import jax
import jax.numpy as jnp
from jax import lax

B_DEV = 16
P_SIZE = 256
K = 64
R = 16
NEAR = 8
M0 = 32
M1 = 32
M2 = 16
LEAVES = 512
POINTS = 131072
PARENTS = 64
GRAND = 8
CAP = 32
NW = 8


def coupling_plan(key):
    shards = LEAVES // B_DEV
    slot_total = B_DEV * M0
    busiest = jax.random.randint(jax.random.fold_in(key, 11), (), 0, shards)
    subkeys = jax.random.split(jax.random.fold_in(key, 12), shards)
    ranking = jax.vmap(lambda subkey: jax.random.permutation(subkey, slot_total))(subkeys)
    forced = ranking < CAP
    peer_index = jax.random.randint(jax.random.fold_in(key, 13), (shards, slot_total), 0, shards - 1)
    peer_index = jnp.where(peer_index >= busiest, peer_index + 1, peer_index)
    peer_index = jnp.where(forced, busiest, peer_index)
    kept_slots = (jax.random.randint(jax.random.fold_in(key, 14), (shards, slot_total), 0, 10) < 9) | forced
    onehot = ((peer_index[:, :, None] == jnp.arange(shards, dtype=jnp.int32)[None, None, :]) & kept_slots[:, :, None]).astype(jnp.int32)
    before = jnp.cumsum(onehot, axis=1) - onehot
    arrival = jnp.sum(before * onehot, axis=2)
    kept_slots = kept_slots & (arrival < CAP)
    member_leaf = jax.random.randint(jax.random.fold_in(key, 15), (shards, slot_total), 0, B_DEV)
    source = (peer_index * B_DEV + member_leaf).reshape(LEAVES, M0).astype(jnp.int32)
    return (source, kept_slots.reshape(LEAVES, M0).astype(jnp.int32))


def near_plan(key):
    target = jnp.arange(LEAVES, dtype=jnp.int32)[:, None]
    offset = jax.random.randint(jax.random.fold_in(key, 21), (LEAVES, NEAR), -NW, NW + 1)
    chosen = jax.random.randint(jax.random.fold_in(key, 22), (LEAVES, 1), 0, NEAR)
    edge_offset = jnp.where(target % 2 == 0, NW, -NW)
    edge_slot = jnp.arange(NEAR, dtype=jnp.int32)[None, :] == chosen
    offset = jnp.where(edge_slot, edge_offset, offset)
    source = jnp.clip(target + offset, 0, LEAVES - 1).astype(jnp.int32)
    valid_slots = (jax.random.randint(jax.random.fold_in(key, 23), (LEAVES, NEAR), 0, 4) < 3) | edge_slot
    return (source, valid_slots.astype(jnp.int32))


def draw_leaf_source(key, part):
    source, valid_slots = coupling_plan(key)
    return source


def draw_leaf_valid(key, part):
    source, valid_slots = coupling_plan(key)
    return valid_slots


def draw_near_source(key, part):
    source, valid_slots = near_plan(key)
    return source


def draw_near_valid(key, part):
    source, valid_slots = near_plan(key)
    return valid_slots


def plant(entries, rng, smallest, high):
    spot = [jax.random.randint(jax.random.fold_in(rng, axis), (), 0, length) for axis, length in enumerate(entries.shape)]
    main_axis = entries.shape.index(max(entries.shape))
    neighbour = spot[:main_axis] + [(spot[main_axis] + 1) % entries.shape[main_axis]] + spot[main_axis + 1:]
    return entries.at[tuple(spot)].set(smallest).at[tuple(neighbour)].set(high)


def block_levels(key, shape, cuts, low, top_value):
    gain, own = 1.0, jax.random.fold_in(key, 6)
    for position, parts in cuts:
        draws = jnp.exp(jax.random.uniform(jax.random.fold_in(own, position), (parts,), jnp.float32, low / len(cuts), top_value / len(cuts)))
        gain = gain * jnp.repeat(draws, shape[position] // parts).reshape([-1 if axis == position else 1 for axis in range(len(shape))])
    return gain


def scatter_about(own_key, extent, spread, limit, cuts=(), held_as=jnp.bfloat16):
    values = spread * jax.random.normal(own_key, extent, jnp.float32)
    if cuts:
        values = values * block_levels(own_key, extent, cuts, -0.22, 0.18)
    return jnp.clip(values, -limit, limit).astype(held_as)


def setup_inputs(seed: int = 0) -> dict:
    splits = jax.random.split(jax.random.key(seed), 17)
    densities = scatter_about(splits[0], (R, POINTS), 1.0, 6.0, ((1, 32),))
    basis = scatter_about(splits[1], (LEAVES, K, P_SIZE), P_SIZE ** -0.5, 0.375, ((0, 32),))
    near_blocks = scatter_about(splits[2], (LEAVES, NEAR * P_SIZE, P_SIZE), (NEAR * P_SIZE) ** -0.5, 0.125, ((0, 32),))
    near_source = draw_near_source(jax.random.fold_in(splits[16], 71), 0)
    near_valid = draw_near_valid(jax.random.fold_in(splits[16], 71), 0)
    leaf_coupling = scatter_about(splits[5], (LEAVES, K, M0 * K), (M0 * K) ** -0.5, 0.125, ((0, 32),))
    leaf_source = draw_leaf_source(jax.random.fold_in(splits[16], 71), 0)
    leaf_valid = draw_leaf_valid(jax.random.fold_in(splits[16], 71), 0)
    parent_transfer = scatter_about(splits[8], (PARENTS, K, 8 * K), (3 * K) ** -0.5, 0.4375, ((0, 32),))
    parent_coupling = scatter_about(splits[9], (PARENTS, K, M1 * K), (M1 * K) ** -0.5, 0.125, ((0, 32),))
    parent_source = plant(jax.random.randint(splits[10], (PARENTS, M1), 0, PARENTS), jax.random.fold_in(splits[10], 1), 0, PARENTS - 1).astype(jnp.int32)
    parent_valid = plant((jax.random.randint(splits[11], (PARENTS, M1), 0, 4) < 3).astype(jnp.int32), jax.random.fold_in(splits[11], 1), 0, 1)
    grand_transfer = scatter_about(splits[12], (GRAND, K, 8 * K), (3 * K) ** -0.5, 0.4375)
    grand_coupling = scatter_about(splits[13], (GRAND, K, M2 * K), (M2 * K) ** -0.5, 0.1875, ((0, 8),))
    grand_source = plant(jax.random.randint(splits[14], (GRAND, M2), 0, GRAND), jax.random.fold_in(splits[14], 1), 0, GRAND - 1).astype(jnp.int32)
    grand_valid = plant((jax.random.randint(splits[15], (GRAND, M2), 0, 4) < 3).astype(jnp.int32), jax.random.fold_in(splits[15], 1), 0, 1)
    return {"densities": densities, "basis": basis, "near_blocks": near_blocks, "near_source": near_source, "near_valid": near_valid, "leaf_coupling": leaf_coupling, "leaf_source": leaf_source, "leaf_valid": leaf_valid, "parent_transfer": parent_transfer, "parent_coupling": parent_coupling, "parent_source": parent_source, "parent_valid": parent_valid, "grand_transfer": grand_transfer, "grand_coupling": grand_coupling, "grand_source": grand_source, "grand_valid": grand_valid}


def blockwise(function, operands, total):
    group_size = math.gcd(total, 64)
    shaped = tuple(operand.reshape((total // group_size, group_size) + operand.shape[1:]) for operand in operands)
    result = lax.map(function, shaped)
    return result.reshape((total,) + result.shape[2:])


def couple(coefficients, source, valid_slots, blocks):
    rank_width = coefficients.shape[-1]

    def one_block(operands):
        block_source, block_valid, block_moves = operands
        picked = jnp.take(coefficients, block_source, axis=0)
        picked = jnp.where(block_valid[:, :, None, None] == 1, picked, jnp.zeros((), coefficients.dtype))
        coupling_view = block_moves.reshape(block_moves.shape[0], rank_width, block_source.shape[1], rank_width)
        return jnp.einsum('tjrb,tajb->tra', picked.astype(jnp.float32), coupling_view.astype(jnp.float32))

    return blockwise(one_block, (source, valid_slots, blocks), source.shape[0])


def reference(densities, basis, near_blocks, near_source, near_valid, leaf_coupling, leaf_source, leaf_valid, parent_transfer, parent_coupling, parent_source, parent_valid, grand_transfer, grand_coupling, grand_source, grand_valid):
    right_sides = densities.shape[0]
    leaves, rank_width, leaf_width = basis.shape
    parents = leaves // 8
    grands = parents // 8
    blocked = densities.reshape(right_sides, leaves, leaf_width)
    upward = jnp.einsum('rtp,tkp->trk', blocked.astype(jnp.float32), basis.astype(jnp.float32)).astype(jnp.bfloat16)
    children = upward.reshape(parents, 8, right_sides, rank_width)
    parent_up = jnp.einsum('pcrb,pkcb->prk', children.astype(jnp.float32), parent_transfer.reshape(parents, rank_width, 8, rank_width).astype(jnp.float32)).astype(jnp.bfloat16)
    grand_children = parent_up.reshape(grands, 8, right_sides, rank_width)
    grand_up = jnp.einsum('gcrb,gkcb->grk', grand_children.astype(jnp.float32), grand_transfer.reshape(grands, rank_width, 8, rank_width).astype(jnp.float32)).astype(jnp.bfloat16)
    leaf_far = couple(upward, leaf_source, leaf_valid, leaf_coupling)
    parent_far = couple(parent_up, parent_source, parent_valid, parent_coupling)
    grand_total = couple(grand_up, grand_source, grand_valid, grand_coupling).astype(jnp.bfloat16)
    down_two = jnp.einsum('grk,gkm->grm', grand_total.astype(jnp.float32), grand_transfer.astype(jnp.float32))
    down_two = down_two.reshape(grands, right_sides, 8, rank_width).transpose(0, 2, 1, 3).reshape(parents, right_sides, rank_width)
    parent_total = (parent_far + down_two).astype(jnp.bfloat16)
    down_one = jnp.einsum('prk,pkm->prm', parent_total.astype(jnp.float32), parent_transfer.astype(jnp.float32))
    down_one = down_one.reshape(parents, right_sides, 8, rank_width).transpose(0, 2, 1, 3).reshape(leaves, right_sides, rank_width)
    leaf_total = (leaf_far + down_one).astype(jnp.bfloat16)

    def near_block(operands):
        block_source, block_valid, block_dense, block_basis, block_total = operands
        picked = jnp.take(blocked, block_source, axis=1)
        picked = jnp.where(block_valid[None, :, :, None] == 1, picked, jnp.zeros((), blocked.dtype))
        picked = picked.reshape(right_sides, block_source.shape[0], -1)
        near_field = jnp.einsum('rtm,tmq->trq', picked.astype(jnp.float32), block_dense.astype(jnp.float32))
        far_field = jnp.einsum('trk,tkq->trq', block_total.astype(jnp.float32), block_basis.astype(jnp.float32))
        return far_field + near_field

    summed = blockwise(near_block, (near_source, near_valid, near_blocks, basis, leaf_total), leaves)
    return summed.astype(jnp.bfloat16).transpose(1, 0, 2).reshape(right_sides, leaves * leaf_width)
```

```python
import functools

import jax
import jax.numpy as jnp
from jax import lax
from jax.experimental import pallas as pl
from jax.experimental.pallas import tpu as pltpu
from jax.sharding import PartitionSpec as P

BF16 = jnp.bfloat16
F32 = jnp.float32
CORES = 2
LANES = 128


def dot_nt(a, b):
    return lax.dot_general(a, b, (((1,), (1,)), ((), ())), preferred_element_type=F32)


def dot_nn(a, b):
    return lax.dot_general(a, b, (((1,), (0,)), ((), ())), preferred_element_type=F32)


def fused_kernel(
    groups,
    subs,
    near_source,
    near_valid,
    leaf_source,
    leaf_valid,
    parent_source,
    parent_valid,
    grand_source,
    grand_valid,
    densities,
    basis,
    near_blocks,
    leaf_coupling,
    parent_transfer,
    parent_coupling,
    grand_transfer,
    grand_coupling,
    out,
    padded,
    slabs,
    basis_v,
    near_v,
    coupling_v,
    transfer_v,
    parent_coupling_v,
    grand_transfer_v,
    grand_coupling_v,
    table,
    leaf_rows,
    parent_rows,
    grand_rows,
    near_sum,
    leaf_far,
    load_sem,
    near_sem,
    coupling_sem,
    halo_send,
    halo_recv,
    line_send,
    line_recv,
    plane_send,
    plane_recv,
    twin_send,
    twin_recv,
):
    rs = densities.shape[0]
    pairs, pair_rank, width = basis.shape
    leaves = 2 * pairs
    rank = pair_rank // 2
    reach = leaves // 2
    near_slots = near_source.shape[1]
    leaf_slots = leaf_source.shape[1]
    grand_slots = grand_source.shape[1]
    total_devices = groups * subs
    total_leaves = total_devices * leaves
    total_parents = total_devices * 2
    chips = groups // CORES
    low = lax.broadcasted_iota(jnp.int32, (rs, LANES), 1) < rank

    group = lax.axis_index("leaf")
    sub = lax.axis_index("sub")
    me = group * subs + sub
    chip = group // CORES
    core = group % CORES
    following = (me + 1) % total_devices
    previous = (me + total_devices - 1) % total_devices
    following = (following // subs, following % subs)
    previous = (previous // subs, previous % subs)
    twin = (chip * CORES + (1 - core), sub)

    def line(i):
        return (group, (sub + i) % subs)

    def plane(k):
        return (((chip + k) % chips) * CORES + core, sub)

    reach_width = reach * width
    own_width = leaves * width
    loads = [
        pltpu.make_async_copy(
            densities, padded.at[:, reach_width : reach_width + own_width], load_sem.at[0]
        ),
        pltpu.make_async_copy(basis, basis_v, load_sem.at[1]),
        pltpu.make_async_copy(parent_transfer, transfer_v, load_sem.at[2]),
        pltpu.make_async_copy(grand_transfer, grand_transfer_v, load_sem.at[3]),
        pltpu.make_async_copy(parent_coupling, parent_coupling_v, load_sem.at[4]),
        pltpu.make_async_copy(grand_coupling, grand_coupling_v, load_sem.at[5]),
    ]

    def near_load(t):
        return pltpu.make_async_copy(near_blocks.at[t], near_v.at[t], near_sem.at[t])

    def coupling_load(i):
        return pltpu.make_async_copy(leaf_coupling.at[i], coupling_v.at[i], coupling_sem.at[i])

    for load in loads[:3]:
        load.start()

    barrier = pltpu.get_barrier_semaphore()
    partners = [following, previous, twin]
    partners += [line(i) for i in range(1, subs)] + [plane(k) for k in range(1, chips)]
    for partner in partners:
        pl.semaphore_signal(
            barrier, inc=1, device_id=partner, device_id_type=pl.DeviceIdType.MESH
        )

    lax.fori_loop(0, leaves, lambda t, c: (near_load(t).start(), c)[1], 0)
    for load in loads[3:]:
        load.start()
    lax.fori_loop(0, pairs, lambda i, c: (coupling_load(i).start(), c)[1], 0)

    slabs[leaves + 2 * reach] = jnp.zeros((rs, width), BF16)
    leaf_rows[total_leaves] = jnp.zeros((rs, LANES), BF16)
    parent_rows[total_parents] = jnp.zeros((rs, LANES), BF16)
    grand_rows[groups] = jnp.zeros((rs, LANES), BF16)

    pl.semaphore_wait(barrier, len(partners))

    def remote(src, dst, send, recv, device):
        return pltpu.make_async_remote_copy(
            src_ref=src,
            dst_ref=dst,
            send_sem=send,
            recv_sem=recv,
            device_id=device,
            device_id_type=pl.DeviceIdType.MESH,
        )

    halo = [
        remote(
            densities.at[:, own_width - reach_width :],
            padded.at[:, :reach_width],
            halo_send.at[0],
            halo_recv.at[0],
            following,
        ),
        remote(
            densities.at[:, :reach_width],
            padded.at[:, reach_width + own_width :],
            halo_send.at[1],
            halo_recv.at[1],
            previous,
        ),
    ]
    for copy in halo:
        copy.start()

    for load in loads[:3]:
        load.wait()

    def tile_of(both):
        return jnp.where(low, both[:rs], both[rs:])

    own = table.at[group, sub]
    tiles = []
    for i in range(pairs):
        start = reach_width + 2 * i * width
        two = jnp.concatenate(
            [padded[:, start : start + width], padded[:, start + width : start + 2 * width]], axis=0
        )
        tile = tile_of(dot_nt(two, basis_v[i])).astype(BF16)
        own[i] = tile
        tiles.append(tile)
    children = jnp.concatenate(
        [jnp.concatenate(tiles[:4], axis=1), jnp.concatenate(tiles[4:], axis=1)], axis=0
    )
    own[pairs] = tile_of(dot_nt(children, transfer_v[...])).astype(BF16)

    def line_copy(i):
        block = table.at[group, sub]
        return remote(block, block, line_send.at[i], line_recv.at[i], line(i))

    def plane_copy(i, k):
        block = table.at[group, (sub + subs - i) % subs]
        return remote(block, block, plane_send.at[i, k], plane_recv.at[i, k], plane(k))

    def twin_copy(i, k):
        block = table.at[((chip + chips - k) % chips) * CORES + core, (sub + subs - i) % subs]
        return remote(block, block, twin_send.at[i, k], twin_recv.at[i, k], twin)

    def spread(i):
        if i > 0:
            line_copy(i).wait_recv()
        for k in range(1, chips):
            plane_copy(i, k).start()
        twin_copy(i, 0).start()

    def pass_on(i):
        for k in range(1, chips):
            plane_copy(i, k).wait_recv()
            twin_copy(i, k).start()

    for i in range(1, subs):
        line_copy(i).start()
    spread(0)

    def choose(valid, source, missing):
        return missing + valid * (source - missing)

    base = me * leaves - reach

    def near_step(t, carry):
        near_load(t).wait()
        total = jnp.zeros((rs, width), F32)
        for j in range(near_slots):
            place = choose(near_valid[t, j], near_source[t, j] - base, leaves + 2 * reach)
            total += dot_nn(slabs[place], near_v[t, j * width : (j + 1) * width, :])
        near_sum[:, pl.ds(pl.multiple_of(t * width, width), width)] = total
        return carry

    for copy in halo:
        copy.wait()
    for i in range(leaves + 2 * reach):
        slabs[i] = padded[:, i * width : (i + 1) * width]
    cuts = [0]
    for i in range(1, subs):
        cuts.append(leaves * i // (2 * subs) + 1)
        lax.fori_loop(cuts[-2], cuts[-1], near_step, 0)
        spread(i)
    for i in range(subs):
        cuts.append(leaves if i == subs - 1 else cuts[-1] + (leaves - cuts[-1]) // (subs - i))
        lax.fori_loop(cuts[-2], cuts[-1], near_step, 0)
        pass_on(i)
    for i in range(subs):
        for k in range(chips):
            twin_copy(i, k).wait_recv()

    def duplicate(tile):
        turned = jnp.concatenate([tile[:, rank:], tile[:, :rank]], axis=1)
        return jnp.where(low, tile, turned), jnp.where(low, turned, tile)

    def unpack(d, carry):
        g, s = d // subs, d % subs
        for i in range(pairs):
            first, second = duplicate(table[g, s, i])
            leaf_rows[d * leaves + 2 * i] = first
            leaf_rows[d * leaves + 2 * i + 1] = second
        first, second = duplicate(table[g, s, pairs])
        parent_rows[2 * d] = first
        parent_rows[2 * d + 1] = second
        return carry

    lax.fori_loop(0, total_devices, unpack, 0)

    def gather(rows, source, valid, t, slots, missing):
        parts = []
        for j in range(0, slots, 2):
            a = rows[choose(valid[t, j], source[t, j], missing)]
            b = rows[choose(valid[t, j + 1], source[t, j + 1], missing)]
            parts.append(jnp.where(low, a, b))
        return jnp.concatenate(parts, axis=1)

    for load in loads[3:]:
        load.wait()

    def lift(g, carry):
        up = jnp.concatenate([table[g, s, pairs] for s in range(subs)], axis=1)
        up = dot_nt(up, grand_transfer_v[g]).astype(BF16)
        grand_rows[g] = jnp.concatenate([up, up], axis=1)
        return carry

    lax.fori_loop(0, groups, lift, 0)
    picked = gather(grand_rows, grand_source, grand_valid, 0, grand_slots, groups)
    grand_total = dot_nt(picked, grand_coupling_v[0]).astype(BF16)
    parent_lanes = pl.ds(pl.multiple_of(sub * LANES, LANES), LANES)
    down_two = dot_nn(grand_total, grand_transfer_v[group, :, parent_lanes])

    def pair_far(rows, source, valid, t, missing, blocks):
        two = jnp.concatenate(
            [gather(rows, source, valid, t + h, leaf_slots, missing) for h in range(2)], axis=0
        )
        return tile_of(dot_nt(two, blocks))

    parent_far = pair_far(
        parent_rows, parent_source, parent_valid, 0, total_parents, parent_coupling_v[...]
    )
    parent_total = (parent_far + down_two).astype(BF16)
    nothing = jnp.zeros((rs, LANES), BF16)

    def split(tile):
        return jnp.concatenate(
            [jnp.where(low, tile, nothing), jnp.where(low, nothing, tile)], axis=0
        )

    down_one = dot_nn(split(parent_total), transfer_v[...])
    half = pairs // 2
    for i in range(pairs):
        row = (i // half) * rs
        lane = (i % half) * LANES
        leaf_far[i] = down_one[row : row + rs, lane : lane + LANES]

    def leaf_step(i, carry):
        coupling_load(i).wait()
        far = pair_far(leaf_rows, leaf_source, leaf_valid, 2 * i, total_leaves, coupling_v[i])
        leaf_total = (far + leaf_far[i]).astype(BF16)
        both = dot_nn(split(leaf_total), basis_v[i])
        for h in range(2):
            lanes = pl.ds(pl.multiple_of((2 * i + h) * width, width), width)
            out[:, lanes] = (both[h * rs : (h + 1) * rs] + near_sum[:, lanes]).astype(BF16)
        return carry

    lax.fori_loop(0, pairs, leaf_step, 0)

    for i in range(1, subs):
        line_copy(i).wait_send()
    for i in range(subs):
        for k in range(chips):
            if k > 0:
                plane_copy(i, k).wait_send()
            twin_copy(i, k).wait_send()


def body(
    groups,
    subs,
    densities,
    basis,
    near_blocks,
    near_source,
    near_valid,
    leaf_coupling,
    leaf_source,
    leaf_valid,
    parent_transfer,
    parent_coupling,
    parent_source,
    parent_valid,
    grand_transfer,
    grand_coupling,
    grand_source,
    grand_valid,
):
    rs = densities.shape[0]
    leaves, rank, width = basis.shape
    pairs = leaves // 2
    devices = groups * subs
    chips = groups // CORES
    basis = basis.reshape(pairs, 2 * rank, width)
    leaf_coupling = leaf_coupling.reshape(pairs, 2 * rank, leaf_coupling.shape[2])
    parent_transfer = parent_transfer.reshape(2 * rank, parent_transfer.shape[2])
    parent_coupling = parent_coupling.reshape(2 * rank, parent_coupling.shape[2])
    smem = pl.BlockSpec(memory_space=pltpu.SMEM)
    anywhere = pl.BlockSpec(memory_space=pl.ANY)
    dma = pltpu.SemaphoreType.DMA
    return pl.pallas_call(
        functools.partial(fused_kernel, groups, subs),
        out_shape=jax.ShapeDtypeStruct(densities.shape, BF16),
        in_specs=[smem] * 8 + [anywhere] * 8,
        out_specs=pl.BlockSpec(memory_space=pltpu.VMEM),
        scratch_shapes=[
            pltpu.VMEM((rs, 2 * leaves * width), BF16),
            pltpu.VMEM((2 * leaves + 1, rs, width), BF16),
            pltpu.VMEM(basis.shape, BF16),
            pltpu.VMEM(near_blocks.shape, BF16),
            pltpu.VMEM(leaf_coupling.shape, BF16),
            pltpu.VMEM(parent_transfer.shape, BF16),
            pltpu.VMEM(parent_coupling.shape, BF16),
            pltpu.VMEM(grand_transfer.shape, BF16),
            pltpu.VMEM(grand_coupling.shape, BF16),
            pltpu.VMEM((groups, subs, pairs + 1, rs, LANES), BF16),
            pltpu.VMEM((devices * leaves + 1, rs, LANES), BF16),
            pltpu.VMEM((devices * 2 + 1, rs, LANES), BF16),
            pltpu.VMEM((groups + 1, rs, LANES), BF16),
            pltpu.VMEM((rs, leaves * width), F32),
            pltpu.VMEM((pairs, rs, LANES), F32),
            dma((6,)),
            dma((leaves,)),
            dma((pairs,)),
            dma((2,)),
            dma((2,)),
            dma((subs,)),
            dma((subs,)),
            dma((subs, chips)),
            dma((subs, chips)),
            dma((subs, chips)),
            dma((subs, chips)),
        ],
        compiler_params=pltpu.CompilerParams(
            collective_id=0, has_side_effects=True, vmem_limit_bytes=52 * 1024 * 1024
        ),
        cost_estimate=pl.CostEstimate(
            flops=2 * rs * near_blocks.size, bytes_accessed=2 * near_blocks.size, transcendentals=0
        ),
    )(
        near_source,
        near_valid,
        leaf_source,
        leaf_valid,
        parent_source,
        parent_valid,
        grand_source,
        grand_valid,
        densities,
        basis,
        near_blocks,
        leaf_coupling,
        parent_transfer,
        parent_coupling,
        grand_transfer,
        grand_coupling,
    )


def solution(mesh):
    both = ("leaf", "sub")
    return jax.shard_map(
        functools.partial(body, mesh.shape["leaf"], mesh.shape["sub"]),
        mesh=mesh,
        in_specs=(
            P(None, both),
            P(both, None, None),
            P(both, None, None),
            P(both, None),
            P(both, None),
            P(both, None, None),
            P(both, None),
            P(both, None),
            P(both, None, None),
            P(both, None, None),
            P(both, None),
            P(both, None),
            P(),
            P("leaf", None, None),
            P("leaf", None),
            P("leaf", None),
        ),
        out_specs=P(None, both),
        check_vma=False,
    )
```

```python
import functools

import jax
import jax.numpy as jnp
from jax import lax
from jax.experimental import pallas as pl
from jax.experimental.pallas import tpu as pltpu
from jax.sharding import PartitionSpec as P

BF16 = jnp.bfloat16
F32 = jnp.float32
CORES = 2
LANES = 128


def dot_nt(a, b):
    return lax.dot_general(a, b, (((1,), (1,)), ((), ())), preferred_element_type=F32)


def dot_nn(a, b):
    return lax.dot_general(a, b, (((1,), (0,)), ((), ())), preferred_element_type=F32)


def fused_kernel(
    groups,
    subs,
    *refs,
):
    lists, refs = refs[:8], refs[8:]
    (
    densities,
    basis,
    near_blocks,
    leaf_coupling,
    parent_transfer,
    parent_coupling,
    grand_transfer,
    grand_coupling,
    out,
    padded,
    slabs,
    basis_v,
    near_v,
    coupling_v,
    transfer_v,
    parent_coupling_v,
    grand_transfer_v,
    grand_coupling_v,
    table,
    leaf_rows,
    parent_rows,
    grand_rows,
    near_sum,
    load_sem,
    near_sem,
    coupling_sem,
    halo_send,
    halo_recv,
    line_send,
    line_recv,
    plane_send,
    plane_recv,
    twin_send,
    twin_recv,
    list_sem,
    place_sem,
    ), refs = refs[:36], refs[36:]
    lists_v, places_v, places = refs[:8], refs[8:12], refs[12:]
    near_place, leaf_place, parent_place, grand_place = places
    rs = densities.shape[0]
    pairs, pair_rank, width = basis.shape
    leaves = 2 * pairs
    rank = pair_rank // 2
    reach = leaves // 2
    near_slots = lists[0].shape[0]
    leaf_slots = lists[2].shape[1]
    grand_slots = lists[6].shape[1]
    total_devices = groups * subs
    total_leaves = total_devices * leaves
    total_parents = total_devices * 2
    chips = groups // CORES
    low = lax.broadcasted_iota(jnp.int32, (rs, LANES), 1) < rank

    group = lax.axis_index("leaf")
    sub = lax.axis_index("sub")
    me = group * subs + sub
    chip = group // CORES
    core = group % CORES
    following = (me + 1) % total_devices
    previous = (me + total_devices - 1) % total_devices
    following = (following // subs, following % subs)
    previous = (previous // subs, previous % subs)
    twin = (chip * CORES + (1 - core), sub)

    def line(i):
        return (group, (sub + i) % subs)

    def plane(k):
        return (((chip + k) % chips) * CORES + core, sub)

    reach_width = reach * width
    own_width = leaves * width
    loads = [
        pltpu.make_async_copy(
            densities, padded.at[:, reach_width : reach_width + own_width], load_sem.at[0]
        ),
        pltpu.make_async_copy(basis, basis_v, load_sem.at[1]),
        pltpu.make_async_copy(parent_transfer, transfer_v, load_sem.at[2]),
        pltpu.make_async_copy(grand_transfer, grand_transfer_v, load_sem.at[3]),
        pltpu.make_async_copy(parent_coupling, parent_coupling_v, load_sem.at[4]),
        pltpu.make_async_copy(grand_coupling, grand_coupling_v, load_sem.at[5]),
    ]

    list_loads = [
        pltpu.make_async_copy(lists[n], lists_v[n], list_sem.at[n]) for n in range(8)
    ]
    place_loads = [
        pltpu.make_async_copy(places_v[n], places[n], place_sem.at[n]) for n in range(4)
    ]

    def near_load(i):
        both = pl.ds(2 * i, 2)
        return pltpu.make_async_copy(near_blocks.at[both], near_v.at[both], near_sem.at[i])

    def coupling_load(i):
        return pltpu.make_async_copy(leaf_coupling.at[i], coupling_v.at[i], coupling_sem.at[i])

    for load in loads[:3] + list_loads:
        load.start()

    barrier = pltpu.get_barrier_semaphore()
    partners = [following, previous, twin]
    partners += [line(i) for i in range(1, subs)] + [plane(k) for k in range(1, chips)]
    for partner in partners:
        pl.semaphore_signal(
            barrier, inc=1, device_id=partner, device_id_type=pl.DeviceIdType.MESH
        )

    lax.fori_loop(0, pairs, lambda i, c: (near_load(i).start(), c)[1], 0)
    for load in loads[3:]:
        load.start()
    lax.fori_loop(0, pairs, lambda i, c: (coupling_load(i).start(), c)[1], 0)

    slabs[leaves + 2 * reach] = jnp.zeros((rs, width), BF16)
    leaf_rows[total_leaves] = jnp.zeros((rs, LANES), BF16)
    parent_rows[total_parents] = jnp.zeros((rs, LANES), BF16)
    grand_rows[groups] = jnp.zeros((rs, LANES), BF16)

    for load in list_loads:
        load.wait()
    firsts = [me * leaves - reach, 0, 0, 0]
    zeros = [leaves + 2 * reach, total_leaves, total_parents, groups]
    for n in range(4):
        source, valid = lists_v[2 * n][...], lists_v[2 * n + 1][...]
        places_v[n][...] = jnp.where(valid == 1, source - firsts[n], zeros[n])
        place_loads[n].start()

    pl.semaphore_wait(barrier, len(partners))

    def remote(src, dst, send, recv, device):
        return pltpu.make_async_remote_copy(
            src_ref=src,
            dst_ref=dst,
            send_sem=send,
            recv_sem=recv,
            device_id=device,
            device_id_type=pl.DeviceIdType.MESH,
        )

    halo = [
        remote(
            densities.at[:, own_width - reach_width :],
            padded.at[:, :reach_width],
            halo_send.at[0],
            halo_recv.at[0],
            following,
        ),
        remote(
            densities.at[:, :reach_width],
            padded.at[:, reach_width + own_width :],
            halo_send.at[1],
            halo_recv.at[1],
            previous,
        ),
    ]
    for copy in halo:
        copy.start()

    for load in loads[:3]:
        load.wait()

    def tile_of(both):
        return jnp.where(low, both[:rs], both[rs:])

    own = table.at[group, sub]
    tiles = []
    for i in range(pairs):
        start = reach_width + 2 * i * width
        two = jnp.concatenate(
            [padded[:, start : start + width], padded[:, start + width : start + 2 * width]], axis=0
        )
        tile = tile_of(dot_nt(two, basis_v[i])).astype(BF16)
        own[i] = tile
        tiles.append(tile)
    children = jnp.concatenate(
        [jnp.concatenate(tiles[:4], axis=1), jnp.concatenate(tiles[4:], axis=1)], axis=0
    )
    own[pairs] = tile_of(dot_nt(children, transfer_v[...])).astype(BF16)

    def line_copy(i):
        block = table.at[group, sub]
        return remote(block, block, line_send.at[i], line_recv.at[i], line(i))

    def plane_copy(i, k):
        block = table.at[group, (sub + subs - i) % subs]
        return remote(block, block, plane_send.at[i, k], plane_recv.at[i, k], plane(k))

    def twin_copy(i, k):
        block = table.at[((chip + chips - k) % chips) * CORES + core, (sub + subs - i) % subs]
        return remote(block, block, twin_send.at[i, k], twin_recv.at[i, k], twin)

    def spread(i):
        if i > 0:
            line_copy(i).wait_recv()
        for k in range(1, chips):
            plane_copy(i, k).start()
        twin_copy(i, 0).start()

    def pass_on(i):
        for k in range(1, chips):
            plane_copy(i, k).wait_recv()
            twin_copy(i, k).start()

    for i in range(1, subs):
        line_copy(i).start()
    spread(0)

    def near_step(i, carry):
        near_load(i).wait()
        sums = [jnp.zeros((rs, width), F32) for h in range(2)]
        for j in range(near_slots):
            for h in range(2):
                t = 2 * i + h
                rows = near_v[t, j * width : (j + 1) * width, :]
                sums[h] += dot_nn(slabs[near_place[j, t]], rows)
        lanes = pl.ds(pl.multiple_of(2 * i * width, 2 * width), 2 * width)
        near_sum[:, lanes] = jnp.concatenate(sums, axis=1)
        return carry

    for copy in halo:
        copy.wait()
    for load in place_loads:
        load.wait()
    for i in range(leaves + 2 * reach):
        slabs[i] = padded[:, i * width : (i + 1) * width]
    cuts = [0]
    for i in range(1, subs):
        cuts.append(pairs * i // (2 * subs) + 1)
        lax.fori_loop(cuts[-2], cuts[-1], near_step, 0)
        spread(i)
    for i in range(subs):
        cuts.append(pairs if i == subs - 1 else cuts[-1] + (pairs - cuts[-1]) // (subs - i))
        lax.fori_loop(cuts[-2], cuts[-1], near_step, 0)
        pass_on(i)

    def duplicate(tile):
        turned = jnp.concatenate([tile[:, rank:], tile[:, :rank]], axis=1)
        return jnp.where(low, tile, turned), jnp.where(low, turned, tile)

    def unpack(column, s):
        d = column * subs + s
        for i in range(pairs):
            first, second = duplicate(table[column, s, i])
            leaf_rows[d * leaves + 2 * i] = first
            leaf_rows[d * leaves + 2 * i + 1] = second
        first, second = duplicate(table[column, s, pairs])
        parent_rows[2 * d] = first
        parent_rows[2 * d + 1] = second

    for i in range(subs):
        for k in range(chips):
            unpack(((chip + chips - k) % chips) * CORES + core, (sub + subs - i) % subs)
    for i in range(subs):
        for k in range(chips):
            twin_copy(i, k).wait_recv()
            unpack(((chip + chips - k) % chips) * CORES + 1 - core, (sub + subs - i) % subs)

    def gather(rows, place, t, slots):
        parts = []
        for j in range(0, slots, 2):
            parts.append(jnp.where(low, rows[place[t, j]], rows[place[t, j + 1]]))
        return jnp.concatenate(parts, axis=1)

    for load in loads[3:]:
        load.wait()
    for i in range(pairs):
        coupling_load(i).wait()

    for g in range(groups):
        up = jnp.concatenate([table[g, s, pairs] for s in range(subs)], axis=1)
        up = dot_nt(up, grand_transfer_v[g]).astype(BF16)
        grand_rows[g] = jnp.concatenate([up, up], axis=1)
    picked = gather(grand_rows, grand_place, 0, grand_slots)
    grand_total = dot_nt(picked, grand_coupling_v[0]).astype(BF16)
    parent_lanes = pl.ds(pl.multiple_of(sub * LANES, LANES), LANES)
    down_two = dot_nn(grand_total, grand_transfer_v[group, :, parent_lanes])

    def pair_far(rows, place, i, blocks):
        two = [gather(rows, place, 2 * i + h, leaf_slots) for h in range(2)]
        return tile_of(dot_nt(jnp.concatenate(two, axis=0), blocks))

    parent_far = pair_far(parent_rows, parent_place, 0, parent_coupling_v[...])
    parent_total = (parent_far + down_two).astype(BF16)
    nothing = jnp.zeros((rs, LANES), BF16)

    def split(tile):
        return jnp.concatenate(
            [jnp.where(low, tile, nothing), jnp.where(low, nothing, tile)], axis=0
        )

    down_one = dot_nn(split(parent_total), transfer_v[...])
    half = pairs // 2

    for i in range(pairs):
        row, lane = (i // half) * rs, (i % half) * LANES
        far = pair_far(leaf_rows, leaf_place, i, coupling_v[i])
        leaf_total = (far + down_one[row : row + rs, lane : lane + LANES]).astype(BF16)
        both = dot_nn(split(leaf_total), basis_v[i])
        for h in range(2):
            start = (2 * i + h) * width
            summed = both[h * rs : (h + 1) * rs] + near_sum[:, start : start + width]
            out[:, start : start + width] = summed.astype(BF16)

    for i in range(1, subs):
        line_copy(i).wait_send()
    for i in range(subs):
        for k in range(chips):
            if k > 0:
                plane_copy(i, k).wait_send()
            twin_copy(i, k).wait_send()


def body(
    groups,
    subs,
    densities,
    basis,
    near_blocks,
    near_source,
    near_valid,
    leaf_coupling,
    leaf_source,
    leaf_valid,
    parent_transfer,
    parent_coupling,
    parent_source,
    parent_valid,
    grand_transfer,
    grand_coupling,
    grand_source,
    grand_valid,
):
    rs = densities.shape[0]
    leaves, rank, width = basis.shape
    pairs = leaves // 2
    devices = groups * subs
    chips = groups // CORES
    basis = basis.reshape(pairs, 2 * rank, width)
    leaf_coupling = leaf_coupling.reshape(pairs, 2 * rank, leaf_coupling.shape[2])
    parent_transfer = parent_transfer.reshape(2 * rank, parent_transfer.shape[2])
    parent_coupling = parent_coupling.reshape(2 * rank, parent_coupling.shape[2])
    lists = [
        near_source.T,
        near_valid.T,
        leaf_source,
        leaf_valid,
        parent_source,
        parent_valid,
        grand_source,
        grand_valid,
    ]
    anywhere = pl.BlockSpec(memory_space=pl.ANY)
    dma = pltpu.SemaphoreType.DMA
    return pl.pallas_call(
        functools.partial(fused_kernel, groups, subs),
        out_shape=jax.ShapeDtypeStruct(densities.shape, BF16),
        in_specs=[anywhere] * 16,
        out_specs=pl.BlockSpec(memory_space=pltpu.VMEM),
        scratch_shapes=[
            pltpu.VMEM((rs, 2 * leaves * width), BF16),
            pltpu.VMEM((2 * leaves + 1, rs, width), BF16),
            pltpu.VMEM(basis.shape, BF16),
            pltpu.VMEM(near_blocks.shape, BF16),
            pltpu.VMEM(leaf_coupling.shape, BF16),
            pltpu.VMEM(parent_transfer.shape, BF16),
            pltpu.VMEM(parent_coupling.shape, BF16),
            pltpu.VMEM(grand_transfer.shape, BF16),
            pltpu.VMEM(grand_coupling.shape, BF16),
            pltpu.VMEM((groups, subs, pairs + 1, rs, LANES), BF16),
            pltpu.VMEM((devices * leaves + 1, rs, LANES), BF16),
            pltpu.VMEM((devices * 2 + 1, rs, LANES), BF16),
            pltpu.VMEM((groups + 1, rs, LANES), BF16),
            pltpu.VMEM((rs, leaves * width), F32),
            dma((6,)),
            dma((pairs,)),
            dma((pairs,)),
            dma((2,)),
            dma((2,)),
            dma((subs,)),
            dma((subs,)),
            dma((subs, chips)),
            dma((subs, chips)),
            dma((subs, chips)),
            dma((subs, chips)),
            dma((8,)),
            dma((4,)),
        ]
        + [pltpu.VMEM(entries.shape, jnp.int32) for entries in lists]
        + [pltpu.VMEM(entries.shape, jnp.int32) for entries in lists[::2]]
        + [pltpu.SMEM(entries.shape, jnp.int32) for entries in lists[::2]],
        compiler_params=pltpu.CompilerParams(
            collective_id=0, has_side_effects=True, vmem_limit_bytes=64 * 1024 * 1024
        ),
        cost_estimate=pl.CostEstimate(
            flops=2 * rs * near_blocks.size, bytes_accessed=2 * near_blocks.size, transcendentals=0
        ),
    )(
        *lists,
        densities,
        basis,
        near_blocks,
        leaf_coupling,
        parent_transfer,
        parent_coupling,
        grand_transfer,
        grand_coupling,
    )


def solution(mesh):
    both = ("leaf", "sub")
    return jax.shard_map(
        functools.partial(body, mesh.shape["leaf"], mesh.shape["sub"]),
        mesh=mesh,
        in_specs=(
            P(None, both),
            P(both, None, None),
            P(both, None, None),
            P(both, None),
            P(both, None),
            P(both, None, None),
            P(both, None),
            P(both, None),
            P(both, None, None),
            P(both, None, None),
            P(both, None),
            P(both, None),
            P(),
            P("leaf", None, None),
            P("leaf", None),
            P("leaf", None),
        ),
        out_specs=P(None, both),
        check_vma=False,
    )
```

```python
import functools

import jax
import jax.numpy as jnp
from jax import lax
from jax.experimental import pallas as pl
from jax.experimental.pallas import tpu as pltpu
from jax.sharding import PartitionSpec as P

BF16 = jnp.bfloat16
F32 = jnp.float32
CORES = 2
LANES = 128


def dot_nt(a, b):
    return lax.dot_general(a, b, (((1,), (1,)), ((), ())), preferred_element_type=F32)


def dot_nn(a, b):
    return lax.dot_general(a, b, (((1,), (0,)), ((), ())), preferred_element_type=F32)


def near_kernel(
    groups,
    subs,
    near_source,
    near_valid,
    densities,
    basis,
    near_blocks,
    parent_transfer,
    out_table,
    out_near,
    padded,
    slabs,
    basis_v,
    near_v,
    transfer_v,
    table,
    near_sum,
    source_v,
    valid_v,
    place_v,
    near_place,
    load_sem,
    near_sem,
    halo_send,
    halo_recv,
    line_send,
    line_recv,
    plane_send,
    plane_recv,
    twin_send,
    twin_recv,
    keep_sem,
):
    rs = densities.shape[0]
    pairs, pair_rank, width = basis.shape
    leaves = 2 * pairs
    rank = pair_rank // 2
    reach = leaves // 2
    near_slots = near_source.shape[0]
    total_devices = groups * subs
    chips = groups // CORES
    low = lax.broadcasted_iota(jnp.int32, (rs, LANES), 1) < rank

    group = lax.axis_index("leaf")
    sub = lax.axis_index("sub")
    me = group * subs + sub
    chip = group // CORES
    core = group % CORES
    following = (me + 1) % total_devices
    previous = (me + total_devices - 1) % total_devices
    following = (following // subs, following % subs)
    previous = (previous // subs, previous % subs)
    twin = (chip * CORES + (1 - core), sub)

    def line(i):
        return (group, (sub + i) % subs)

    def plane(k):
        return (((chip + k) % chips) * CORES + core, sub)

    reach_width = reach * width
    own_width = leaves * width
    loads = [
        pltpu.make_async_copy(
            densities, padded.at[:, reach_width : reach_width + own_width], load_sem.at[0]
        ),
        pltpu.make_async_copy(basis, basis_v, load_sem.at[1]),
        pltpu.make_async_copy(parent_transfer, transfer_v, load_sem.at[2]),
        pltpu.make_async_copy(near_source, source_v, load_sem.at[3]),
        pltpu.make_async_copy(near_valid, valid_v, load_sem.at[4]),
    ]
    place_load = pltpu.make_async_copy(place_v, near_place, load_sem.at[5])

    def near_load(i):
        both = pl.ds(2 * i, 2)
        return pltpu.make_async_copy(near_blocks.at[both], near_v.at[both], near_sem.at[i])

    for load in loads:
        load.start()

    barrier = pltpu.get_barrier_semaphore()
    partners = [following, previous, twin]
    partners += [line(i) for i in range(1, subs)] + [plane(k) for k in range(1, chips)]
    for partner in partners:
        pl.semaphore_signal(
            barrier, inc=1, device_id=partner, device_id_type=pl.DeviceIdType.MESH
        )

    lax.fori_loop(0, pairs, lambda i, c: (near_load(i).start(), c)[1], 0)
    slabs[leaves + 2 * reach] = jnp.zeros((rs, width), BF16)

    for load in loads[3:]:
        load.wait()
    local = source_v[...] - (me * leaves - reach)
    place_v[...] = jnp.where(valid_v[...] == 1, local, leaves + 2 * reach)
    place_load.start()

    pl.semaphore_wait(barrier, len(partners))

    def remote(src, dst, send, recv, device):
        return pltpu.make_async_remote_copy(
            src_ref=src,
            dst_ref=dst,
            send_sem=send,
            recv_sem=recv,
            device_id=device,
            device_id_type=pl.DeviceIdType.MESH,
        )

    halo = [
        remote(
            densities.at[:, own_width - reach_width :],
            padded.at[:, :reach_width],
            halo_send.at[0],
            halo_recv.at[0],
            following,
        ),
        remote(
            densities.at[:, :reach_width],
            padded.at[:, reach_width + own_width :],
            halo_send.at[1],
            halo_recv.at[1],
            previous,
        ),
    ]
    for copy in halo:
        copy.start()

    for load in loads[:3]:
        load.wait()

    def tile_of(both):
        return jnp.where(low, both[:rs], both[rs:])

    own = table.at[group, sub]
    tiles = []
    for i in range(pairs):
        start = reach_width + 2 * i * width
        two = jnp.concatenate(
            [padded[:, start : start + width], padded[:, start + width : start + 2 * width]], axis=0
        )
        tile = tile_of(dot_nt(two, basis_v[i])).astype(BF16)
        own[i] = tile
        tiles.append(tile)
    children = jnp.concatenate(
        [jnp.concatenate(tiles[:4], axis=1), jnp.concatenate(tiles[4:], axis=1)], axis=0
    )
    own[pairs] = tile_of(dot_nt(children, transfer_v[...])).astype(BF16)

    def line_copy(i):
        block = table.at[group, sub]
        return remote(block, block, line_send.at[i], line_recv.at[i], line(i))

    def plane_copy(i, k):
        block = table.at[group, (sub + subs - i) % subs]
        return remote(block, block, plane_send.at[i, k], plane_recv.at[i, k], plane(k))

    def twin_copy(i, k):
        block = table.at[((chip + chips - k) % chips) * CORES + core, (sub + subs - i) % subs]
        return remote(block, block, twin_send.at[i, k], twin_recv.at[i, k], twin)

    def spread(i):
        if i > 0:
            line_copy(i).wait_recv()
        for k in range(1, chips):
            plane_copy(i, k).start()
        twin_copy(i, 0).start()

    def pass_on(i):
        for k in range(1, chips):
            plane_copy(i, k).wait_recv()
            twin_copy(i, k).start()

    for i in range(1, subs):
        line_copy(i).start()
    spread(0)

    def near_step(i, carry):
        near_load(i).wait()
        sums = [jnp.zeros((rs, width), F32) for h in range(2)]
        for j in range(near_slots):
            for h in range(2):
                t = 2 * i + h
                rows = near_v[t, j * width : (j + 1) * width, :]
                sums[h] += dot_nn(slabs[near_place[j, t]], rows)
        lanes = pl.ds(pl.multiple_of(2 * i * width, 2 * width), 2 * width)
        near_sum[:, lanes] = jnp.concatenate(sums, axis=1)
        return carry

    for copy in halo:
        copy.wait()
    place_load.wait()
    for i in range(leaves + 2 * reach):
        slabs[i] = padded[:, i * width : (i + 1) * width]
    cuts = [0]
    for i in range(1, subs):
        cuts.append(pairs * i // (2 * subs) + 1)
        lax.fori_loop(cuts[-2], cuts[-1], near_step, 0)
        spread(i)
    for i in range(subs):
        cuts.append(pairs if i == subs - 1 else cuts[-1] + (pairs - cuts[-1]) // (subs - i))
        lax.fori_loop(cuts[-2], cuts[-1], near_step, 0)
        pass_on(i)

    def keep(i, k, other):
        column = ((chip + chips - k) % chips) * CORES + (1 - core if other else core)
        block = (column, (sub + subs - i) % subs)
        n = 2 * (i * chips + k) + int(other)
        return pltpu.make_async_copy(table.at[block], out_table.at[block], keep_sem.at[n])

    sums_out = pltpu.make_async_copy(near_sum, out_near, load_sem.at[3])
    sums_out.start()
    blocks = [(i, k) for i in range(subs) for k in range(chips)]
    for i, k in blocks:
        keep(i, k, False).start()
    for i, k in blocks:
        twin_copy(i, k).wait_recv()
        keep(i, k, True).start()
    for i, k in blocks:
        keep(i, k, False).wait()
        keep(i, k, True).wait()
    sums_out.wait()

    for i in range(1, subs):
        line_copy(i).wait_send()
    for i in range(subs):
        for k in range(chips):
            if k > 0:
                plane_copy(i, k).wait_send()
            twin_copy(i, k).wait_send()


def far_kernel(groups, subs, *refs):
    lists, refs = refs[:6], refs[6:]
    (
        table_h,
        near_h,
        basis,
        leaf_coupling,
        parent_transfer,
        parent_coupling,
        grand_transfer,
        grand_coupling,
        out,
        table,
        near_sum,
        basis_v,
        coupling_v,
        transfer_v,
        parent_coupling_v,
        grand_transfer_v,
        grand_coupling_v,
        leaf_rows,
        parent_rows,
        grand_rows,
        load_sem,
        table_sem,
        coupling_sem,
        list_sem,
        place_sem,
    ) = refs[:25]
    lists_v, places_v, places = refs[25:31], refs[31:34], refs[34:]
    leaf_place, parent_place, grand_place = places
    pairs, pair_rank, width = basis.shape
    rs = near_h.shape[0]
    leaves = 2 * pairs
    rank = pair_rank // 2
    leaf_slots = lists[0].shape[1]
    grand_slots = lists[4].shape[1]
    total_leaves = groups * subs * leaves
    total_parents = groups * subs * 2
    low = lax.broadcasted_iota(jnp.int32, (rs, LANES), 1) < rank
    group = lax.axis_index("leaf")
    sub = lax.axis_index("sub")

    def tile_of(both):
        return jnp.where(low, both[:rs], both[rs:])

    held = [
        (grand_transfer, grand_transfer_v),
        (grand_coupling, grand_coupling_v),
        (parent_coupling, parent_coupling_v),
        (parent_transfer, transfer_v),
        (basis, basis_v),
        (near_h, near_sum),
    ]
    loads = [pltpu.make_async_copy(a, b, load_sem.at[n]) for n, (a, b) in enumerate(held)]
    list_loads = [
        pltpu.make_async_copy(lists[n], lists_v[n], list_sem.at[n]) for n in range(6)
    ]
    place_loads = [
        pltpu.make_async_copy(places_v[n], places[n], place_sem.at[n]) for n in range(3)
    ]

    def table_load(column):
        return pltpu.make_async_copy(table_h.at[column], table.at[column], table_sem.at[column])

    def coupling_load(i):
        return pltpu.make_async_copy(leaf_coupling.at[i], coupling_v.at[i], coupling_sem.at[i])

    for load in list_loads + [table_load(column) for column in range(groups)] + loads:
        load.start()
    for i in range(pairs):
        coupling_load(i).start()
    leaf_rows[total_leaves] = jnp.zeros((rs, LANES), BF16)
    parent_rows[total_parents] = jnp.zeros((rs, LANES), BF16)
    grand_rows[groups] = jnp.zeros((rs, LANES), BF16)

    for load in list_loads:
        load.wait()
    zeros = [total_leaves, total_parents, groups]
    for n in range(3):
        places_v[n][...] = jnp.where(lists_v[2 * n + 1][...] == 1, lists_v[2 * n][...], zeros[n])
        place_loads[n].start()

    def duplicate(tile):
        turned = jnp.concatenate([tile[:, rank:], tile[:, :rank]], axis=1)
        return jnp.where(low, tile, turned), jnp.where(low, turned, tile)

    def unpack(column, s):
        d = column * subs + s
        for i in range(pairs):
            first, second = duplicate(table[column, s, i])
            leaf_rows[d * leaves + 2 * i] = first
            leaf_rows[d * leaves + 2 * i + 1] = second
        first, second = duplicate(table[column, s, pairs])
        parent_rows[2 * d] = first
        parent_rows[2 * d + 1] = second

    for column in range(groups):
        table_load(column).wait()
        for s in range(subs):
            unpack(column, s)
    for load in place_loads:
        load.wait()

    def gather(rows, place, t, slots):
        parts = []
        for j in range(0, slots, 2):
            parts.append(jnp.where(low, rows[place[t, j]], rows[place[t, j + 1]]))
        return jnp.concatenate(parts, axis=1)

    for load in loads:
        load.wait()
    for i in range(pairs):
        coupling_load(i).wait()

    for g in range(groups):
        up = jnp.concatenate([table[g, s, pairs] for s in range(subs)], axis=1)
        up = dot_nt(up, grand_transfer_v[g]).astype(BF16)
        grand_rows[g] = jnp.concatenate([up, up], axis=1)
    picked = gather(grand_rows, grand_place, 0, grand_slots)
    grand_total = dot_nt(picked, grand_coupling_v[0]).astype(BF16)
    parent_lanes = pl.ds(pl.multiple_of(sub * LANES, LANES), LANES)
    down_two = dot_nn(grand_total, grand_transfer_v[group, :, parent_lanes])

    def pair_far(rows, place, i, blocks):
        two = [gather(rows, place, 2 * i + h, leaf_slots) for h in range(2)]
        return tile_of(dot_nt(jnp.concatenate(two, axis=0), blocks))

    parent_far = pair_far(parent_rows, parent_place, 0, parent_coupling_v[...])
    parent_total = (parent_far + down_two).astype(BF16)
    nothing = jnp.zeros((rs, LANES), BF16)

    def split(tile):
        return jnp.concatenate(
            [jnp.where(low, tile, nothing), jnp.where(low, nothing, tile)], axis=0
        )

    down_one = dot_nn(split(parent_total), transfer_v[...])
    half = pairs // 2

    for i in range(pairs):
        row, lane = (i // half) * rs, (i % half) * LANES
        far = pair_far(leaf_rows, leaf_place, i, coupling_v[i])
        leaf_total = (far + down_one[row : row + rs, lane : lane + LANES]).astype(BF16)
        both = dot_nn(split(leaf_total), basis_v[i])
        for h in range(2):
            start = (2 * i + h) * width
            summed = both[h * rs : (h + 1) * rs] + near_sum[:, start : start + width]
            out[:, start : start + width] = summed.astype(BF16)


def body(
    groups,
    subs,
    densities,
    basis,
    near_blocks,
    near_source,
    near_valid,
    leaf_coupling,
    leaf_source,
    leaf_valid,
    parent_transfer,
    parent_coupling,
    parent_source,
    parent_valid,
    grand_transfer,
    grand_coupling,
    grand_source,
    grand_valid,
):
    rs = densities.shape[0]
    leaves, rank, width = basis.shape
    pairs = leaves // 2
    devices = groups * subs
    chips = groups // CORES
    basis = basis.reshape(pairs, 2 * rank, width)
    leaf_coupling = leaf_coupling.reshape(pairs, 2 * rank, leaf_coupling.shape[2])
    parent_transfer = parent_transfer.reshape(2 * rank, parent_transfer.shape[2])
    parent_coupling = parent_coupling.reshape(2 * rank, parent_coupling.shape[2])
    anywhere = pl.BlockSpec(memory_space=pl.ANY)
    dma = pltpu.SemaphoreType.DMA
    near_lists = near_source.T.shape
    table = (groups, subs, pairs + 1, rs, LANES)
    sums = (rs, leaves * width)
    limit = 64 * 1024 * 1024
    every, near = pl.pallas_call(
        functools.partial(near_kernel, groups, subs),
        out_shape=[jax.ShapeDtypeStruct(table, BF16), jax.ShapeDtypeStruct(sums, F32)],
        in_specs=[anywhere] * 6,
        out_specs=[anywhere] * 2,
        scratch_shapes=[
            pltpu.VMEM((rs, 2 * leaves * width), BF16),
            pltpu.VMEM((2 * leaves + 1, rs, width), BF16),
            pltpu.VMEM(basis.shape, BF16),
            pltpu.VMEM(near_blocks.shape, BF16),
            pltpu.VMEM(parent_transfer.shape, BF16),
            pltpu.VMEM(table, BF16),
            pltpu.VMEM(sums, F32),
            pltpu.VMEM(near_lists, jnp.int32),
            pltpu.VMEM(near_lists, jnp.int32),
            pltpu.VMEM(near_lists, jnp.int32),
            pltpu.SMEM(near_lists, jnp.int32),
            dma((6,)),
            dma((pairs,)),
            dma((2,)),
            dma((2,)),
            dma((subs,)),
            dma((subs,)),
            dma((subs, chips)),
            dma((subs, chips)),
            dma((subs, chips)),
            dma((subs, chips)),
            dma((2 * subs * chips,)),
        ],
        compiler_params=pltpu.CompilerParams(
            collective_id=0, has_side_effects=True, vmem_limit_bytes=limit
        ),
        cost_estimate=pl.CostEstimate(
            flops=2 * rs * near_blocks.size, bytes_accessed=2 * near_blocks.size, transcendentals=0
        ),
    )(near_source.T, near_valid.T, densities, basis, near_blocks, parent_transfer)
    lists = [leaf_source, leaf_valid, parent_source, parent_valid, grand_source, grand_valid]
    return pl.pallas_call(
        functools.partial(far_kernel, groups, subs),
        out_shape=jax.ShapeDtypeStruct(densities.shape, BF16),
        in_specs=[anywhere] * 14,
        out_specs=pl.BlockSpec(memory_space=pltpu.VMEM),
        scratch_shapes=[
            pltpu.VMEM(table, BF16),
            pltpu.VMEM(sums, F32),
            pltpu.VMEM(basis.shape, BF16),
            pltpu.VMEM(leaf_coupling.shape, BF16),
            pltpu.VMEM(parent_transfer.shape, BF16),
            pltpu.VMEM(parent_coupling.shape, BF16),
            pltpu.VMEM(grand_transfer.shape, BF16),
            pltpu.VMEM(grand_coupling.shape, BF16),
            pltpu.VMEM((devices * leaves + 1, rs, LANES), BF16),
            pltpu.VMEM((devices * 2 + 1, rs, LANES), BF16),
            pltpu.VMEM((groups + 1, rs, LANES), BF16),
            dma((6,)),
            dma((groups,)),
            dma((pairs,)),
            dma((6,)),
            dma((3,)),
        ]
        + [pltpu.VMEM(entries.shape, jnp.int32) for entries in lists]
        + [pltpu.VMEM(entries.shape, jnp.int32) for entries in lists[::2]]
        + [pltpu.SMEM(entries.shape, jnp.int32) for entries in lists[::2]],
        compiler_params=pltpu.CompilerParams(vmem_limit_bytes=limit),
        cost_estimate=pl.CostEstimate(
            flops=2 * rs * leaf_coupling.size, bytes_accessed=2 * leaf_coupling.size, transcendentals=0
        ),
    )(
        *lists,
        every,
        near,
        basis,
        leaf_coupling,
        parent_transfer,
        parent_coupling,
        grand_transfer,
        grand_coupling,
    )


def solution(mesh):
    both = ("leaf", "sub")
    return jax.shard_map(
        functools.partial(body, mesh.shape["leaf"], mesh.shape["sub"]),
        mesh=mesh,
        in_specs=(
            P(None, both),
            P(both, None, None),
            P(both, None, None),
            P(both, None),
            P(both, None),
            P(both, None, None),
            P(both, None),
            P(both, None),
            P(both, None, None),
            P(both, None, None),
            P(both, None),
            P(both, None),
            P(),
            P("leaf", None, None),
            P("leaf", None),
            P("leaf", None),
        ),
        out_specs=P(None, both),
        check_vma=False,
    )
```

```python
import functools

import jax
import jax.numpy as jnp
from jax import lax
from jax.experimental import pallas as pl
from jax.experimental.pallas import tpu as pltpu
from jax.sharding import PartitionSpec as P

BF16 = jnp.bfloat16
F32 = jnp.float32
CORES = 2
LANES = 128


def dot_nt(a, b):
    return lax.dot_general(a, b, (((1,), (1,)), ((), ())), preferred_element_type=F32)


def dot_nn(a, b):
    return lax.dot_general(a, b, (((1,), (0,)), ((), ())), preferred_element_type=F32)


def fused_kernel(
    groups,
    subs,
    *refs,
):
    lists, refs = refs[:8], refs[8:]
    (
    densities,
    basis,
    near_blocks,
    leaf_coupling,
    parent_transfer,
    parent_coupling,
    grand_transfer,
    grand_coupling,
    out,
    padded,
    slabs,
    basis_v,
    near_v,
    coupling_v,
    transfer_v,
    parent_coupling_v,
    grand_transfer_v,
    grand_coupling_v,
    table,
    leaf_rows,
    parent_rows,
    grand_rows,
    near_sum,
    load_sem,
    near_sem,
    coupling_sem,
    halo_send,
    halo_recv,
    line_send,
    line_recv,
    plane_send,
    plane_recv,
    twin_send,
    twin_recv,
    list_sem,
    place_sem,
    ), refs = refs[:36], refs[36:]
    lists_v, places_v, places = refs[:8], refs[8:12], refs[12:]
    near_place, leaf_place, parent_place, grand_place = places
    rs = densities.shape[0]
    pairs, pair_rank, width = basis.shape
    leaves = 2 * pairs
    rank = pair_rank // 2
    reach = leaves // 2
    near_slots = lists[0].shape[0]
    leaf_slots = lists[2].shape[1]
    grand_slots = lists[6].shape[1]
    total_devices = groups * subs
    total_leaves = total_devices * leaves
    total_parents = total_devices * 2
    chips = groups // CORES
    low = lax.broadcasted_iota(jnp.int32, (rs, LANES), 1) < rank

    group = lax.axis_index("leaf")
    sub = lax.axis_index("sub")
    me = group * subs + sub
    chip = group // CORES
    core = group % CORES
    following = (me + 1) % total_devices
    previous = (me + total_devices - 1) % total_devices
    following = (following // subs, following % subs)
    previous = (previous // subs, previous % subs)
    twin = (chip * CORES + (1 - core), sub)

    def line(i):
        return (group, (sub + i) % subs)

    def plane(k):
        return (((chip + k) % chips) * CORES + core, sub)

    reach_width = reach * width
    own_width = leaves * width
    loads = [
        pltpu.make_async_copy(
            densities, padded.at[:, reach_width : reach_width + own_width], load_sem.at[0]
        ),
        pltpu.make_async_copy(basis, basis_v, load_sem.at[1]),
        pltpu.make_async_copy(parent_transfer, transfer_v, load_sem.at[2]),
        pltpu.make_async_copy(grand_transfer, grand_transfer_v, load_sem.at[3]),
        pltpu.make_async_copy(parent_coupling, parent_coupling_v, load_sem.at[4]),
        pltpu.make_async_copy(grand_coupling, grand_coupling_v, load_sem.at[5]),
    ]

    list_loads = [
        pltpu.make_async_copy(lists[n], lists_v[n], list_sem.at[n]) for n in range(8)
    ]
    place_loads = [
        pltpu.make_async_copy(places_v[n], places[n], place_sem.at[n]) for n in range(4)
    ]

    def near_load(i):
        both = pl.ds(2 * i, 2)
        return pltpu.make_async_copy(near_blocks.at[both], near_v.at[both], near_sem.at[i])

    def coupling_load(i):
        return pltpu.make_async_copy(leaf_coupling.at[i], coupling_v.at[i], coupling_sem.at[i])

    for load in loads[:3] + list_loads:
        load.start()

    barrier = pltpu.get_barrier_semaphore()
    partners = [following, previous, twin]
    partners += [line(i) for i in range(1, subs)] + [plane(k) for k in range(1, chips)]
    for partner in partners:
        pl.semaphore_signal(
            barrier, inc=1, device_id=partner, device_id_type=pl.DeviceIdType.MESH
        )

    lax.fori_loop(0, pairs, lambda i, c: (near_load(i).start(), c)[1], 0)
    for load in loads[3:]:
        load.start()
    lax.fori_loop(0, pairs, lambda i, c: (coupling_load(i).start(), c)[1], 0)

    slabs[leaves + 2 * reach] = jnp.zeros((rs, width), BF16)
    leaf_rows[total_leaves] = jnp.zeros((rs, LANES), BF16)
    parent_rows[total_parents] = jnp.zeros((rs, LANES), BF16)
    grand_rows[groups] = jnp.zeros((rs, LANES), BF16)

    pl.semaphore_wait(barrier, len(partners))

    def remote(src, dst, send, recv, device):
        return pltpu.make_async_remote_copy(
            src_ref=src,
            dst_ref=dst,
            send_sem=send,
            recv_sem=recv,
            device_id=device,
            device_id_type=pl.DeviceIdType.MESH,
        )

    halo = [
        remote(
            padded.at[:, own_width : reach_width + own_width],
            padded.at[:, :reach_width],
            halo_send.at[0],
            halo_recv.at[0],
            following,
        ),
        remote(
            padded.at[:, reach_width : 2 * reach_width],
            padded.at[:, reach_width + own_width :],
            halo_send.at[1],
            halo_recv.at[1],
            previous,
        ),
    ]
    loads[0].wait()
    for copy in halo:
        copy.start()

    for load in loads[1:3]:
        load.wait()

    def tile_of(both):
        return jnp.where(low, both[:rs], both[rs:])

    own = table.at[group, sub]
    tiles = []
    for i in range(pairs):
        start = reach_width + 2 * i * width
        two = jnp.concatenate(
            [padded[:, start : start + width], padded[:, start + width : start + 2 * width]], axis=0
        )
        tile = tile_of(dot_nt(two, basis_v[i])).astype(BF16)
        own[i] = tile
        tiles.append(tile)
    children = jnp.concatenate(
        [jnp.concatenate(tiles[:4], axis=1), jnp.concatenate(tiles[4:], axis=1)], axis=0
    )
    own[pairs] = tile_of(dot_nt(children, transfer_v[...])).astype(BF16)

    def line_copy(i):
        block = table.at[group, sub]
        return remote(block, block, line_send.at[i], line_recv.at[i], line(i))

    def plane_copy(i, k):
        block = table.at[group, (sub + subs - i) % subs]
        return remote(block, block, plane_send.at[i, k], plane_recv.at[i, k], plane(k))

    def twin_copy(i, k):
        block = table.at[((chip + chips - k) % chips) * CORES + core, (sub + subs - i) % subs]
        return remote(block, block, twin_send.at[i, k], twin_recv.at[i, k], twin)

    def spread(i):
        if i > 0:
            line_copy(i).wait_recv()
        for k in range(1, chips):
            plane_copy(i, k).start()
        twin_copy(i, 0).start()

    def pass_on(i):
        for k in range(1, chips):
            plane_copy(i, k).wait_recv()
            twin_copy(i, k).start()

    for i in range(1, subs):
        line_copy(i).start()
    spread(0)

    for load in list_loads:
        load.wait()
    firsts = [me * leaves - reach, 0, 0, 0]
    zeros = [leaves + 2 * reach, total_leaves, total_parents, groups]
    for n in range(4):
        source, valid = lists_v[2 * n][...], lists_v[2 * n + 1][...]
        places_v[n][...] = jnp.where(valid == 1, source - firsts[n], zeros[n])
        place_loads[n].start()

    def duplicate(tile):
        turned = jnp.concatenate([tile[:, rank:], tile[:, :rank]], axis=1)
        return jnp.where(low, tile, turned), jnp.where(low, turned, tile)

    def unpack(i, k, other):
        column = ((chip + chips - k) % chips) * CORES + (1 - core if other else core)
        s = (sub + subs - i) % subs
        d = column * subs + s
        for n in range(pairs):
            first, second = duplicate(table[column, s, n])
            leaf_rows[d * leaves + 2 * n] = first
            leaf_rows[d * leaves + 2 * n + 1] = second
        first, second = duplicate(table[column, s, pairs])
        parent_rows[2 * d] = first
        parent_rows[2 * d + 1] = second

    def near_step(i):
        near_load(i).wait()
        for t in (2 * i, 2 * i + 1):
            picked = [slabs[near_place[j, t]] for j in range(near_slots)]
            total = dot_nn(jnp.concatenate(picked, axis=1), near_v[t])
            near_sum[:, t * width : (t + 1) * width] = total

    def twin_wait(i):
        for k in range(chips):
            twin_copy(i, k).wait_recv()

    for copy in halo:
        copy.wait()
    for load in place_loads:
        load.wait()
    for i in range(leaves + 2 * reach):
        slabs[i] = padded[:, i * width : (i + 1) * width]
    actions = [(1, i) for i in range(1, subs)] + [(2, i) for i in range(subs)]
    for n in range(max(pairs, len(actions))):
        if n < pairs:
            near_step(n)
        if n < len(actions):
            kind, i = actions[n]
            if kind == 1:
                spread(i)
                unpack(i - 1, 0, False)
            else:
                pass_on(i)
                if i == 0:
                    unpack(subs - 1, 0, False)
                if i >= 2:
                    twin_wait(i - 2)
                for k in range(chips):
                    if k > 0:
                        unpack(i, k, False)
                    if i >= 2:
                        unpack(i - 2, k, True)
    for i in range(max(subs - 2, 0), subs):
        twin_wait(i)
    for i in range(max(subs - 2, 0), subs):
        for k in range(chips):
            unpack(i, k, True)

    def gather(rows, place, t, slots):
        parts = []
        for j in range(0, slots, 2):
            parts.append(jnp.where(low, rows[place[t, j]], rows[place[t, j + 1]]))
        return jnp.concatenate(parts, axis=1)

    for load in loads[3:]:
        load.wait()
    for i in range(pairs):
        coupling_load(i).wait()

    for g in range(groups):
        up = jnp.concatenate([table[g, s, pairs] for s in range(subs)], axis=1)
        up = dot_nt(up, grand_transfer_v[g]).astype(BF16)
        grand_rows[g] = jnp.concatenate([up, up], axis=1)
    picked = gather(grand_rows, grand_place, 0, grand_slots)
    grand_total = dot_nt(picked, grand_coupling_v[0]).astype(BF16)
    parent_lanes = pl.ds(pl.multiple_of(sub * LANES, LANES), LANES)
    down_two = dot_nn(grand_total, grand_transfer_v[group, :, parent_lanes])

    def pair_far(rows, place, i, blocks):
        two = [gather(rows, place, 2 * i + h, leaf_slots) for h in range(2)]
        return tile_of(dot_nt(jnp.concatenate(two, axis=0), blocks))

    parent_far = pair_far(parent_rows, parent_place, 0, parent_coupling_v[...])
    parent_total = (parent_far + down_two).astype(BF16)
    nothing = jnp.zeros((rs, LANES), BF16)

    def split(tile):
        return jnp.concatenate(
            [jnp.where(low, tile, nothing), jnp.where(low, nothing, tile)], axis=0
        )

    down_one = dot_nn(split(parent_total), transfer_v[...])
    half = pairs // 2

    for i in range(pairs):
        row, lane = (i // half) * rs, (i % half) * LANES
        far = pair_far(leaf_rows, leaf_place, i, coupling_v[i])
        leaf_total = (far + down_one[row : row + rs, lane : lane + LANES]).astype(BF16)
        both = dot_nn(split(leaf_total), basis_v[i])
        for h in range(2):
            start = (2 * i + h) * width
            summed = both[h * rs : (h + 1) * rs] + near_sum[:, start : start + width]
            out[:, start : start + width] = summed

    for i in range(1, subs):
        line_copy(i).wait_send()
    for i in range(subs):
        for k in range(chips):
            if k > 0:
                plane_copy(i, k).wait_send()
            twin_copy(i, k).wait_send()


def body(
    groups,
    subs,
    densities,
    basis,
    near_blocks,
    near_source,
    near_valid,
    leaf_coupling,
    leaf_source,
    leaf_valid,
    parent_transfer,
    parent_coupling,
    parent_source,
    parent_valid,
    grand_transfer,
    grand_coupling,
    grand_source,
    grand_valid,
):
    rs = densities.shape[0]
    leaves, rank, width = basis.shape
    pairs = leaves // 2
    devices = groups * subs
    chips = groups // CORES
    basis = basis.reshape(pairs, 2 * rank, width)
    leaf_coupling = leaf_coupling.reshape(pairs, 2 * rank, leaf_coupling.shape[2])
    parent_transfer = parent_transfer.reshape(2 * rank, parent_transfer.shape[2])
    parent_coupling = parent_coupling.reshape(2 * rank, parent_coupling.shape[2])
    lists = [
        near_source.T,
        near_valid.T,
        leaf_source,
        leaf_valid,
        parent_source,
        parent_valid,
        grand_source,
        grand_valid,
    ]
    anywhere = pl.BlockSpec(memory_space=pl.ANY)
    dma = pltpu.SemaphoreType.DMA
    return pl.pallas_call(
        functools.partial(fused_kernel, groups, subs),
        out_shape=jax.ShapeDtypeStruct(densities.shape, F32),
        in_specs=[anywhere] * 16,
        out_specs=pl.BlockSpec(memory_space=pltpu.VMEM),
        scratch_shapes=[
            pltpu.VMEM((rs, 2 * leaves * width), BF16),
            pltpu.VMEM((2 * leaves + 1, rs, width), BF16),
            pltpu.VMEM(basis.shape, BF16),
            pltpu.VMEM(near_blocks.shape, BF16),
            pltpu.VMEM(leaf_coupling.shape, BF16),
            pltpu.VMEM(parent_transfer.shape, BF16),
            pltpu.VMEM(parent_coupling.shape, BF16),
            pltpu.VMEM(grand_transfer.shape, BF16),
            pltpu.VMEM(grand_coupling.shape, BF16),
            pltpu.VMEM((groups, subs, pairs + 1, rs, LANES), BF16),
            pltpu.VMEM((devices * leaves + 1, rs, LANES), BF16),
            pltpu.VMEM((devices * 2 + 1, rs, LANES), BF16),
            pltpu.VMEM((groups + 1, rs, LANES), BF16),
            pltpu.VMEM((rs, leaves * width), F32),
            dma((6,)),
            dma((pairs,)),
            dma((pairs,)),
            dma((2,)),
            dma((2,)),
            dma((subs,)),
            dma((subs,)),
            dma((subs, chips)),
            dma((subs, chips)),
            dma((subs, chips)),
            dma((subs, chips)),
            dma((8,)),
            dma((4,)),
        ]
        + [pltpu.VMEM(entries.shape, jnp.int32) for entries in lists]
        + [pltpu.VMEM(entries.shape, jnp.int32) for entries in lists[::2]]
        + [pltpu.SMEM(entries.shape, jnp.int32) for entries in lists[::2]],
        compiler_params=pltpu.CompilerParams(
            collective_id=0, has_side_effects=True, vmem_limit_bytes=64 * 1024 * 1024
        ),
        cost_estimate=pl.CostEstimate(
            flops=2 * rs * near_blocks.size, bytes_accessed=2 * near_blocks.size, transcendentals=0
        ),
    )(
        *lists,
        densities,
        basis,
        near_blocks,
        leaf_coupling,
        parent_transfer,
        parent_coupling,
        grand_transfer,
        grand_coupling,
    ).astype(BF16)


def solution(mesh):
    both = ("leaf", "sub")
    return jax.shard_map(
        functools.partial(body, mesh.shape["leaf"], mesh.shape["sub"]),
        mesh=mesh,
        in_specs=(
            P(None, both),
            P(both, None, None),
            P(both, None, None),
            P(both, None),
            P(both, None),
            P(both, None, None),
            P(both, None),
            P(both, None),
            P(both, None, None),
            P(both, None, None),
            P(both, None),
            P(both, None),
            P(),
            P("leaf", None, None),
            P("leaf", None),
            P("leaf", None),
        ),
        out_specs=P(None, both),
        check_vma=False,
    )
```

```python
import functools

import jax
import jax.numpy as jnp
from jax import lax
from jax.experimental import pallas as pl
from jax.experimental.pallas import tpu as pltpu
from jax.sharding import PartitionSpec as P

BF16 = jnp.bfloat16
F32 = jnp.float32
CORES = 2
LANES = 128


def dot_nt(a, b):
    return lax.dot_general(a, b, (((1,), (1,)), ((), ())), preferred_element_type=F32)


def dot_nn(a, b):
    return lax.dot_general(a, b, (((1,), (0,)), ((), ())), preferred_element_type=F32)


def fused_kernel(
    groups,
    subs,
    *refs,
):
    lists, refs = refs[:8], refs[8:]
    (
    densities,
    basis,
    near_blocks,
    leaf_coupling,
    parent_transfer,
    parent_coupling,
    grand_transfer,
    grand_coupling,
    out,
    padded,
    slabs,
    basis_v,
    near_v,
    coupling_v,
    transfer_v,
    parent_coupling_v,
    grand_transfer_v,
    grand_coupling_v,
    table,
    leaf_rows,
    parent_rows,
    grand_rows,
    near_sum,
    load_sem,
    near_sem,
    coupling_sem,
    halo_send,
    halo_recv,
    line_send,
    line_recv,
    plane_send,
    plane_recv,
    twin_send,
    twin_recv,
    list_sem,
    place_sem,
    ), refs = refs[:36], refs[36:]
    lists_v, places_v, places = refs[:8], refs[8:12], refs[12:]
    near_place, leaf_place, parent_place, grand_place = places
    rs = densities.shape[0]
    pairs, pair_rank, width = basis.shape
    leaves = 2 * pairs
    rank = pair_rank // 2
    reach = leaves // 2
    near_slots = lists[0].shape[0]
    leaf_slots = lists[2].shape[1]
    grand_slots = lists[6].shape[1]
    total_devices = groups * subs
    total_leaves = total_devices * leaves
    total_parents = total_devices * 2
    chips = groups // CORES
    low = lax.broadcasted_iota(jnp.int32, (rs, LANES), 1) < rank

    group = lax.axis_index("leaf")
    sub = lax.axis_index("sub")
    me = group * subs + sub
    chip = group // CORES
    core = group % CORES
    following = (me + 1) % total_devices
    previous = (me + total_devices - 1) % total_devices
    following = (following // subs, following % subs)
    previous = (previous // subs, previous % subs)
    twin = (chip * CORES + (1 - core), sub)

    def line(i):
        return (group, (sub + i) % subs)

    def plane(k):
        return (((chip + k) % chips) * CORES + core, sub)

    reach_width = reach * width
    own_width = leaves * width
    loads = [
        pltpu.make_async_copy(
            densities, padded.at[:, reach_width : reach_width + own_width], load_sem.at[0]
        ),
        pltpu.make_async_copy(basis, basis_v, load_sem.at[1]),
        pltpu.make_async_copy(parent_transfer, transfer_v, load_sem.at[2]),
        pltpu.make_async_copy(grand_transfer, grand_transfer_v, load_sem.at[3]),
        pltpu.make_async_copy(parent_coupling, parent_coupling_v, load_sem.at[4]),
        pltpu.make_async_copy(grand_coupling, grand_coupling_v, load_sem.at[5]),
    ]

    list_loads = [
        pltpu.make_async_copy(lists[n], lists_v[n], list_sem.at[n]) for n in range(8)
    ]
    place_loads = [
        pltpu.make_async_copy(places_v[n], places[n], place_sem.at[n]) for n in range(4)
    ]

    def near_load(i):
        both = pl.ds(2 * i, 2)
        return pltpu.make_async_copy(near_blocks.at[both], near_v.at[both], near_sem.at[i])

    def coupling_load(i):
        return pltpu.make_async_copy(leaf_coupling.at[i], coupling_v.at[i], coupling_sem.at[i])

    for load in loads[:3] + list_loads:
        load.start()

    barrier = pltpu.get_barrier_semaphore()
    partners = [following, previous, twin]
    partners += [line(i) for i in range(1, subs)] + [plane(k) for k in range(1, chips)]
    for partner in partners:
        pl.semaphore_signal(
            barrier, inc=1, device_id=partner, device_id_type=pl.DeviceIdType.MESH
        )

    lax.fori_loop(0, pairs, lambda i, c: (near_load(i).start(), c)[1], 0)
    for load in loads[3:]:
        load.start()
    lax.fori_loop(0, pairs, lambda i, c: (coupling_load(i).start(), c)[1], 0)

    slabs[leaves + 2 * reach] = jnp.zeros((rs, width), BF16)
    leaf_rows[total_leaves] = jnp.zeros((rs, LANES), BF16)
    parent_rows[total_parents] = jnp.zeros((rs, LANES), BF16)
    grand_rows[groups] = jnp.zeros((rs, LANES), BF16)

    pl.semaphore_wait(barrier, len(partners))

    def remote(src, dst, send, recv, device):
        return pltpu.make_async_remote_copy(
            src_ref=src,
            dst_ref=dst,
            send_sem=send,
            recv_sem=recv,
            device_id=device,
            device_id_type=pl.DeviceIdType.MESH,
        )

    halo = [
        remote(
            padded.at[:, own_width : reach_width + own_width],
            padded.at[:, :reach_width],
            halo_send.at[0],
            halo_recv.at[0],
            following,
        ),
        remote(
            padded.at[:, reach_width : 2 * reach_width],
            padded.at[:, reach_width + own_width :],
            halo_send.at[1],
            halo_recv.at[1],
            previous,
        ),
    ]
    loads[0].wait()
    for copy in halo:
        copy.start()

    for load in loads[1:3]:
        load.wait()

    def tile_of(both):
        return jnp.where(low, both[:rs], both[rs:])

    own = table.at[group, sub]
    tiles = []
    for i in range(pairs):
        start = reach_width + 2 * i * width
        two = jnp.concatenate(
            [padded[:, start : start + width], padded[:, start + width : start + 2 * width]], axis=0
        )
        tile = tile_of(dot_nt(two, basis_v[i])).astype(BF16)
        own[i] = tile
        tiles.append(tile)
    children = jnp.concatenate(
        [jnp.concatenate(tiles[:4], axis=1), jnp.concatenate(tiles[4:], axis=1)], axis=0
    )
    own[pairs] = tile_of(dot_nt(children, transfer_v[...])).astype(BF16)

    def line_copy(i):
        block = table.at[group, sub]
        return remote(block, block, line_send.at[i], line_recv.at[i], line(i))

    def plane_copy(i, k):
        block = table.at[group, (sub + subs - i) % subs]
        return remote(block, block, plane_send.at[i, k], plane_recv.at[i, k], plane(k))

    def twin_copy(i, k):
        block = table.at[((chip + chips - k) % chips) * CORES + core, (sub + subs - i) % subs]
        return remote(block, block, twin_send.at[i, k], twin_recv.at[i, k], twin)

    def spread(i):
        if i > 0:
            line_copy(i).wait_recv()
        for k in range(1, chips):
            plane_copy(i, k).start()
        twin_copy(i, 0).start()

    def pass_on(i):
        for k in range(1, chips):
            plane_copy(i, k).wait_recv()
            twin_copy(i, k).start()

    for i in range(1, subs):
        line_copy(i).start()
    spread(0)

    for load in list_loads:
        load.wait()
    firsts = [me * leaves - reach, 0, 0, 0]
    zeros = [leaves + 2 * reach, total_leaves, total_parents, groups]
    for n in range(4):
        source, valid = lists_v[2 * n][...], lists_v[2 * n + 1][...]
        places_v[n][...] = jnp.where(valid == 1, source - firsts[n], zeros[n])
        place_loads[n].start()

    def duplicate(tile):
        turned = jnp.concatenate([tile[:, rank:], tile[:, :rank]], axis=1)
        return jnp.where(low, tile, turned), jnp.where(low, turned, tile)

    def unpack(i, k, other):
        column = ((chip + chips - k) % chips) * CORES + (1 - core if other else core)
        s = (sub + subs - i) % subs
        d = column * subs + s
        for n in range(pairs):
            first, second = duplicate(table[column, s, n])
            leaf_rows[d * leaves + 2 * n] = first
            leaf_rows[d * leaves + 2 * n + 1] = second
        first, second = duplicate(table[column, s, pairs])
        parent_rows[2 * d] = first
        parent_rows[2 * d + 1] = second

    def near_step(i):
        near_load(i).wait()
        for t in (2 * i, 2 * i + 1):
            picked = [slabs[near_place[j, t]] for j in range(near_slots)]
            total = dot_nn(jnp.concatenate(picked, axis=1), near_v[t])
            near_sum[:, t * width : (t + 1) * width] = total

    def twin_wait(i):
        for k in range(chips):
            twin_copy(i, k).wait_recv()

    for copy in halo:
        copy.wait()
    for load in place_loads:
        load.wait()
    for i in range(leaves + 2 * reach):
        slabs[i] = padded[:, i * width : (i + 1) * width]
    actions = [(1, i) for i in range(1, subs)] + [(2, i) for i in range(subs)]
    for n in range(max(pairs, len(actions))):
        if n < pairs:
            near_step(n)
        if n < len(actions):
            kind, i = actions[n]
            if kind == 1:
                spread(i)
                unpack(i - 1, 0, False)
            else:
                pass_on(i)
                if i == 0:
                    unpack(subs - 1, 0, False)
                if i >= 2:
                    twin_wait(i - 2)
                for k in range(chips):
                    if k > 0:
                        unpack(i, k, False)
                    if i >= 2:
                        unpack(i - 2, k, True)
    for load in loads[3:]:
        load.wait()
    for i in range(pairs):
        coupling_load(i).wait()
    for i in range(max(subs - 2, 0), subs):
        twin_wait(i)
    for i in range(max(subs - 2, 0), subs):
        for k in range(chips):
            unpack(i, k, True)

    def gather(rows, place, t, slots):
        parts = []
        for j in range(0, slots, 2):
            parts.append(jnp.where(low, rows[place[t, j]], rows[place[t, j + 1]]))
        return jnp.concatenate(parts, axis=1)

    for g in range(groups):
        up = jnp.concatenate([table[g, s, pairs] for s in range(subs)], axis=1)
        up = dot_nt(up, grand_transfer_v[g]).astype(BF16)
        grand_rows[g] = jnp.concatenate([up, up], axis=1)
    picked = gather(grand_rows, grand_place, 0, grand_slots)
    grand_total = dot_nt(picked, grand_coupling_v[0]).astype(BF16)
    parent_lanes = pl.ds(pl.multiple_of(sub * LANES, LANES), LANES)
    down_two = dot_nn(grand_total, grand_transfer_v[group, :, parent_lanes])

    def pair_far(rows, place, i, blocks):
        two = [gather(rows, place, 2 * i + h, leaf_slots) for h in range(2)]
        return tile_of(dot_nt(jnp.concatenate(two, axis=0), blocks))

    parent_far = pair_far(parent_rows, parent_place, 0, parent_coupling_v[...])
    parent_total = (parent_far + down_two).astype(BF16)
    nothing = jnp.zeros((rs, LANES), BF16)

    def split(tile):
        return jnp.concatenate(
            [jnp.where(low, tile, nothing), jnp.where(low, nothing, tile)], axis=0
        )

    down_one = dot_nn(split(parent_total), transfer_v[...])
    half = pairs // 2

    for i in range(pairs):
        row, lane = (i // half) * rs, (i % half) * LANES
        far = pair_far(leaf_rows, leaf_place, i, coupling_v[i])
        leaf_total = (far + down_one[row : row + rs, lane : lane + LANES]).astype(BF16)
        both = dot_nn(split(leaf_total), basis_v[i])
        for h in range(2):
            start = (2 * i + h) * width
            summed = both[h * rs : (h + 1) * rs] + near_sum[:, start : start + width]
            out[:, start : start + width] = summed.astype(BF16)

    for i in range(1, subs):
        line_copy(i).wait_send()
    for i in range(subs):
        for k in range(chips):
            if k > 0:
                plane_copy(i, k).wait_send()
            twin_copy(i, k).wait_send()


def body(
    groups,
    subs,
    densities,
    basis,
    near_blocks,
    near_source,
    near_valid,
    leaf_coupling,
    leaf_source,
    leaf_valid,
    parent_transfer,
    parent_coupling,
    parent_source,
    parent_valid,
    grand_transfer,
    grand_coupling,
    grand_source,
    grand_valid,
):
    rs = densities.shape[0]
    leaves, rank, width = basis.shape
    pairs = leaves // 2
    devices = groups * subs
    chips = groups // CORES
    basis = basis.reshape(pairs, 2 * rank, width)
    leaf_coupling = leaf_coupling.reshape(pairs, 2 * rank, leaf_coupling.shape[2])
    parent_transfer = parent_transfer.reshape(2 * rank, parent_transfer.shape[2])
    parent_coupling = parent_coupling.reshape(2 * rank, parent_coupling.shape[2])
    lists = [
        near_source.T,
        near_valid.T,
        leaf_source,
        leaf_valid,
        parent_source,
        parent_valid,
        grand_source,
        grand_valid,
    ]
    anywhere = pl.BlockSpec(memory_space=pl.ANY)
    dma = pltpu.SemaphoreType.DMA
    return pl.pallas_call(
        functools.partial(fused_kernel, groups, subs),
        out_shape=jax.ShapeDtypeStruct(densities.shape, BF16),
        in_specs=[anywhere] * 16,
        out_specs=pl.BlockSpec(memory_space=pltpu.VMEM),
        scratch_shapes=[
            pltpu.VMEM((rs, 2 * leaves * width), BF16),
            pltpu.VMEM((2 * leaves + 1, rs, width), BF16),
            pltpu.VMEM(basis.shape, BF16),
            pltpu.VMEM(near_blocks.shape, BF16),
            pltpu.VMEM(leaf_coupling.shape, BF16),
            pltpu.VMEM(parent_transfer.shape, BF16),
            pltpu.VMEM(parent_coupling.shape, BF16),
            pltpu.VMEM(grand_transfer.shape, BF16),
            pltpu.VMEM(grand_coupling.shape, BF16),
            pltpu.VMEM((groups, subs, pairs + 1, rs, LANES), BF16),
            pltpu.VMEM((devices * leaves + 1, rs, LANES), BF16),
            pltpu.VMEM((devices * 2 + 1, rs, LANES), BF16),
            pltpu.VMEM((groups + 1, rs, LANES), BF16),
            pltpu.VMEM((rs, leaves * width), F32),
            dma((6,)),
            dma((pairs,)),
            dma((pairs,)),
            dma((2,)),
            dma((2,)),
            dma((subs,)),
            dma((subs,)),
            dma((subs, chips)),
            dma((subs, chips)),
            dma((subs, chips)),
            dma((subs, chips)),
            dma((8,)),
            dma((4,)),
        ]
        + [pltpu.VMEM(entries.shape, jnp.int32) for entries in lists]
        + [pltpu.VMEM(entries.shape, jnp.int32) for entries in lists[::2]]
        + [pltpu.SMEM(entries.shape, jnp.int32) for entries in lists[::2]],
        compiler_params=pltpu.CompilerParams(
            collective_id=0, has_side_effects=True, vmem_limit_bytes=64 * 1024 * 1024
        ),
        cost_estimate=pl.CostEstimate(
            flops=2 * rs * near_blocks.size, bytes_accessed=2 * near_blocks.size, transcendentals=0
        ),
    )(
        *lists,
        densities,
        basis,
        near_blocks,
        leaf_coupling,
        parent_transfer,
        parent_coupling,
        grand_transfer,
        grand_coupling,
    )


def solution(mesh):
    both = ("leaf", "sub")
    return jax.shard_map(
        functools.partial(body, mesh.shape["leaf"], mesh.shape["sub"]),
        mesh=mesh,
        in_specs=(
            P(None, both),
            P(both, None, None),
            P(both, None, None),
            P(both, None),
            P(both, None),
            P(both, None, None),
            P(both, None),
            P(both, None),
            P(both, None, None),
            P(both, None, None),
            P(both, None),
            P(both, None),
            P(),
            P("leaf", None, None),
            P("leaf", None),
            P("leaf", None),
        ),
        out_specs=P(None, both),
        check_vma=False,
    )
```
